32 devices in a mesh: groups: 2 (over y), blk: 4 (over z), width: 4 (over x, core).
Axes of the slice: x: 2, y: 2, z: 4, core: 2. Of those that a mesh axis runs over, the one named last changes fastest.
Arguments:
- t_query: bfloat16 [128, 4096], P(('groups', 'blk'), 'width'), parts along dimension 0
- t_pass: bfloat16 [16384, 4096], P(('groups', 'blk'), 'width'), parts along dimension 0
- s_query: bfloat16 [128, 768], P(('groups', 'blk')), parts along dimension 0
- s_pass: bfloat16 [16384, 768], P(('groups', 'blk', 'width')), parts along dimension 0
- positive: int32 [128], P('groups'), parts along dimension 0, may hold values from 0 to 8191
- doc_ids: int32 [16384], P('groups'), parts along dimension 0, may hold values from 0 to 2047, never falling along the last dimension, each value on 1 to 8 neighbouring positions
Outputs:
- grad_query: float32 [128, 768], P(('groups', 'blk')), parts along dimension 0
- grad_passage: float32 [16384, 768], P(('groups', 'blk', 'width')), parts along dimension 0
The draws below stay inside these ranges and needn't reach their ends.
There are 2 independent parts, one for each index of `groups`. The reference program is written for one: setup_inputs(seed, part) draws one part's arguments, and reference() takes and returns one part's arrays. A program takes and returns all parts, laid end to end along the dimension named above; each array names one. Nothing has to cross between parts.
Inputs may be any that keep to these rules, and one draw needn't show every extreme that they name: `doc_ids`: ids never fall along the passages; at most 8 passages share one.
All inputs are finite; a program needn't handle non-finite values.
Results may differ from the reference program's by a relative error of at most 0.0022.
Values may be sent and summed in bfloat16 or wider, within the bound.
A program may use at most 64 MiB of HBM per device.

```python
import math
import jax
import jax.numpy as jnp
import numpy as np
from jax import lax

T_WIDTH = 4096
S_WIDTH = 768
DOC_MOST = 8
QUERIES = 64
PASSAGES = 8192


TEMPER = 2.0


TARGET_LOGITS = (128.0, 160.0, 208.0, 256.0)


def pairing(key):
    rows = jax.random.permutation(jax.random.fold_in(key, 501), QUERIES)[:4]
    cols = jax.random.randint(jax.random.fold_in(key, 502), (4,), 0, PASSAGES - 1)
    return (rows, cols)


def passage_parts(key, feature_count, salt, nudge):
    rows, cols = pairing(key)
    own_key = jax.random.fold_in(key, salt)
    base_key, scale_key, noise_key = jax.random.split(own_key, 3)
    values = jax.random.normal(base_key, (PASSAGES, feature_count), jnp.float32)
    scales = jnp.exp(jax.random.uniform(scale_key, (PASSAGES,), jnp.float32, math.log(0.7), math.log(2.0)))
    targets = jnp.array(TARGET_LOGITS, jnp.float32)
    spread = 2.0 * TEMPER / targets
    noise = jax.random.normal(noise_key, (4, feature_count), jnp.float32)
    near = values[cols] + spread[:, None] * noise
    values = values.at[cols + 1].set(nudge * near + (1.0 - nudge) * values[cols + 1])
    scales = scales.at[cols + 1].set(nudge * scales[cols] + (1.0 - nudge) * scales[cols + 1])
    return (values, scales)


def query_parts(key, feature_count, salt, passage_salt, nudge):
    own_key = jax.random.fold_in(key, salt)
    base_key, scale_key = jax.random.split(own_key, 2)
    values = jax.random.normal(base_key, (QUERIES, feature_count), jnp.float32)
    scales = jnp.exp(jax.random.uniform(scale_key, (QUERIES,), jnp.float32, math.log(0.5), math.log(5.0)))
    return (values, scales)


def draw_t_pass(key, part):
    values, scales = passage_parts(key, T_WIDTH, 11, 0.0)
    return (values * scales[:, None]).astype(jnp.bfloat16)


def draw_s_pass(key, part):
    values, scales = passage_parts(key, S_WIDTH, 12, 0.0)
    return (values * scales[:, None]).astype(jnp.bfloat16)


def draw_t_query(key, part):
    values, scales = query_parts(key, T_WIDTH, 21, 11, 0.0)
    values = values * scales[:, None]
    return values.astype(jnp.bfloat16)


def draw_s_query(key, part):
    values, scales = query_parts(key, S_WIDTH, 22, 12, 0.0)
    values = values * scales[:, None]
    return values.astype(jnp.bfloat16)


def plant(result, key, smallest, high):
    shape = result.shape
    spot = [jax.random.randint(jax.random.fold_in(key, axis), (), 0, shape[axis]) for axis in range(len(shape))]
    result = result.at[tuple(spot)].set(smallest)
    longest = shape.index(max(shape))
    spot[longest] = (spot[longest] + 1) % shape[longest]
    return result.at[tuple(spot)].set(high)


def length_profile(number_of, total, reach, lean):
    portions = [(1 << 20) // math.isqrt(standing ** lean) + 1 for standing in range(2, number_of + 1)]
    surplus, counts = total - reach - (number_of - 1), [1] * (number_of - 1)
    while surplus > 0:
        candidates = [i for i in range(number_of - 1) if counts[i] < reach]
        whole, budget = sum([portions[i] for i in candidates]), surplus
        for i in candidates:
            extra = min(reach - counts[i], max(1, budget * portions[i] // whole), surplus)
            counts[i] = counts[i] + extra
            surplus = surplus - extra
    return np.array([reach] + counts)


def ragged_sizes(key, count, total, most, lean):
    if count == 2:
        one = jax.random.randint(key, (), max(1, total - most), min(most, total - 1) + 1)
        return jnp.stack([one, total - one])
    tallies = jnp.asarray(length_profile(count, total, most, lean), jnp.int32)
    couples = (count - 1) // 2
    giver, sink = tallies[1:1 + 2 * couples:2], tallies[2:2 + 2 * couples:2]
    margin = jnp.minimum(giver - 1, most - sink)
    shifted = jax.random.randint(jax.random.fold_in(key, 1), (couples,), 0, 1 << 20) % (margin + 1)
    tallies = tallies.at[1:1 + 2 * couples:2].set(giver - shifted).at[2:2 + 2 * couples:2].set(sink + shifted)
    return tallies[jax.random.permutation(jax.random.fold_in(key, 2), count)]


def setup_inputs(seed: int = 0, part: int = 0) -> dict:
    seeds = jax.random.split(jax.random.key(seed), 7)
    part_splits = jax.random.split(jax.random.fold_in(seeds[6], part), 7)
    return {
        "t_query": draw_t_query(jax.random.fold_in(jax.random.fold_in(seeds[6], part), 71), part),
        "t_pass": draw_t_pass(jax.random.fold_in(jax.random.fold_in(seeds[6], part), 71), part),
        "s_query": draw_s_query(jax.random.fold_in(jax.random.fold_in(seeds[6], part), 71), part),
        "s_pass": draw_s_pass(jax.random.fold_in(jax.random.fold_in(seeds[6], part), 71), part),
        "positive": plant(jax.random.randint(part_splits[4], (QUERIES,), 0, PASSAGES), jax.random.fold_in(part_splits[4], 1), 0, PASSAGES - 1).astype(jnp.int32),
        "doc_ids": jnp.searchsorted(jnp.cumsum(ragged_sizes(part_splits[5], PASSAGES // 4, PASSAGES, DOC_MOST, 1)), jnp.arange(PASSAGES), side="right").astype(jnp.int32),
    }


TEMPER = 2.0
MASK_FILL = -1e+30

def softmax_rows(scores, masked):
    filled = jnp.where(masked, MASK_FILL, scores)
    highest = lax.optimization_barrier(jnp.max(filled, axis=1))
    summed = lax.optimization_barrier(jnp.sum(jnp.exp(filled - highest[:, None]), axis=1))
    log_total = highest + jnp.log(summed)
    return jnp.exp(filled - log_total[:, None])

def reference(t_query, t_pass, s_query, s_pass, positive, doc_ids):
    t_scale = TEMPER / math.sqrt(T_WIDTH)
    s_scale = TEMPER / math.sqrt(S_WIDTH)
    teach_logits = jnp.dot(t_query, t_pass.T, preferred_element_type=jnp.float32) * t_scale
    learn_logits = jnp.dot(s_query, s_pass.T, preferred_element_type=jnp.float32) * s_scale
    columns = jnp.arange(PASSAGES, dtype=jnp.int32)
    is_positive = columns[None, :] == positive[:, None]
    target_docs = jnp.take(doc_ids, positive)
    masked = (doc_ids[None, :] == target_docs[:, None]) & jnp.logical_not(is_positive)
    teach_probs = softmax_rows(teach_logits, masked)
    learn_probs = softmax_rows(learn_logits, masked)
    slope = (2.0 * learn_probs - teach_probs - is_positive.astype(jnp.float32)).astype(jnp.bfloat16)
    grad_query = jnp.dot(slope, s_pass, preferred_element_type=jnp.float32) * s_scale
    grad_passage = jnp.dot(slope.T, s_query, preferred_element_type=jnp.float32) * s_scale
    return (grad_query, grad_passage)
```

```python
import functools
import math

import jax
import jax.numpy as jnp
from jax import lax
from jax.experimental import pallas as pl
from jax.experimental.pallas import tpu as pltpu
from jax.sharding import PartitionSpec as P

TEMPER = 2.0
MASK_FILL = -1e30
LANES = 128
MESH_ID = pl.DeviceIdType.MESH
NT = (((1,), (1,)), ((), ()))
TN = (((0,), (0,)), ((), ()))


def kernel(
    sizes,
    tq_ref,
    tp_ref,
    sq_ref,
    sp_ref,
    pos_ref,
    doc_ref,
    gq_ref,
    gp_ref,
    tq_all,
    tp_v,
    sq_all,
    sp_v,
    pos_v,
    doc_v,
    mate_out,
    mate_in,
    far_out,
    far_in,
    stat_w,
    stat_b,
    piece_out,
    piece_in,
    block_out,
    block_in,
    final_in,
    gp_v,
    local_sem,
    tq_send,
    tq_recv,
    sq_send,
    sq_recv,
    mate_send,
    mate_recv,
    far_send,
    far_recv,
    statw_send,
    statw_recv,
    statb_send,
    statb_recv,
    piece_send,
    piece_recv,
    block_send,
    block_recv,
    final_send,
    final_recv,
):
    blocks, widths, t_width, s_width = sizes
    panel = sq_ref.shape[0]
    queries = blocks * panel
    own = sp_ref.shape[0]
    outer = widths // 2
    t_scale = TEMPER / math.sqrt(t_width)
    s_scale = TEMPER / math.sqrt(s_width)
    b = lax.axis_index("blk")
    w = lax.axis_index("width")
    side = lax.rem(w, 2)
    chip = w // 2
    pending = []

    barrier = pltpu.get_barrier_semaphore()
    for k in range(1, blocks):
        pl.semaphore_signal(
            barrier, inc=1, device_id={"blk": lax.rem(b + k, blocks)}, device_id_type=MESH_ID
        )
    for k in range(1, widths):
        pl.semaphore_signal(
            barrier, inc=1, device_id={"width": lax.rem(w + k, widths)}, device_id_type=MESH_ID
        )

    tq_own = pltpu.make_async_copy(tq_ref, tq_all.at[b], local_sem.at[0])
    sq_own = pltpu.make_async_copy(sq_ref, sq_all.at[b], local_sem.at[1])
    sp_copy = pltpu.make_async_copy(sp_ref, sp_v, local_sem.at[2])
    pos_copy = pltpu.make_async_copy(pos_ref, pos_v, local_sem.at[3])
    doc_copy = pltpu.make_async_copy(doc_ref, doc_v, local_sem.at[4])
    tq_own.start()
    sq_own.start()
    pos_copy.start()
    doc_copy.start()
    tp_copies = []
    for step in range(outer):
        target = lax.rem(chip + 1 + step, outer)
        for part in range(2):
            place = 2 * target + (1 - side if part == 0 else side)
            slot = 2 * step + part
            copy = pltpu.make_async_copy(
                tp_ref.at[pl.ds(pl.multiple_of(place * own, own), own), :],
                tp_v.at[slot],
                local_sem.at[5 + slot],
            )
            copy.start()
            tp_copies.append(copy)
    sp_copy.start()

    pl.semaphore_wait(barrier, blocks + widths - 2)

    def send(src, dst, send_sem, recv_sem, where):
        copy = pltpu.make_async_remote_copy(
            src_ref=src,
            dst_ref=dst,
            send_sem=send_sem,
            recv_sem=recv_sem,
            device_id=where,
            device_id_type=MESH_ID,
        )
        copy.start()
        pending.append(copy)
        return copy

    tq_copies, sq_copies = [], []
    for k in range(1, blocks):
        to = {"blk": lax.rem(b + k, blocks)}
        tq_copies.append(send(tq_ref, tq_all.at[b], tq_send.at[k], tq_recv.at[k], to))
    for k in range(1, blocks):
        to = {"blk": lax.rem(b + k, blocks)}
        sq_copies.append(send(sq_ref, sq_all.at[b], sq_send.at[k], sq_recv.at[k], to))

    eye = lax.broadcasted_iota(jnp.int32, (queries, queries), 0) == lax.broadcasted_iota(
        jnp.int32, (queries, queries), 1
    )

    def to_row(column):
        return jnp.sum(jnp.where(eye, column, 0.0), axis=0, keepdims=True)

    def to_column(row):
        return jnp.sum(jnp.where(eye, row, 0.0), axis=1, keepdims=True)

    pos_copy.wait()
    doc_copy.wait()
    positive = to_column(pos_v[...].astype(jnp.float32)).astype(jnp.int32)
    lane = lax.broadcasted_iota(jnp.int32, (1, LANES), 1)

    def look(row, found):
        docs = doc_v[pl.ds(row, 1), :]
        return jnp.where(positive - row * LANES == lane, docs, found)

    found = lax.fori_loop(
        0, doc_v.shape[0], look, jnp.full((queries, LANES), -1, jnp.int32), unroll=4
    )
    target_docs = jnp.max(found.astype(jnp.float32), axis=1, keepdims=True).astype(jnp.int32)
    first_row = (b * widths + w) * own
    first_line = (b * widths + w) * (own // LANES)
    docs = jnp.concatenate(
        [doc_v[pl.ds(first_line + j, 1), :] for j in range(own // LANES)], axis=1
    )
    columns = first_row + lax.broadcasted_iota(jnp.int32, (1, own), 1)
    is_positive = columns == positive
    masked = (docs == target_docs) & jnp.logical_not(is_positive)

    tq_own.wait()
    for copy in tq_copies:
        copy.wait_recv()
    panels = tq_all[...].reshape(queries, tq_all.shape[2])

    def partial_scores(slot):
        tp_copies[slot].wait()
        return lax.dot_general(panels, tp_v[slot], NT, preferred_element_type=jnp.float32)

    teach = None
    far_copies = []
    for step in range(outer):
        mate_out[step] = partial_scores(2 * step)
        mate_copy = send(
            mate_out.at[step],
            mate_in.at[step],
            mate_send.at[step],
            mate_recv.at[step],
            {"width": w + 1 - 2 * side},
        )
        kept = partial_scores(2 * step + 1)
        mate_copy.wait_recv()
        kept = kept + mate_in[step]
        if step < outer - 1:
            far_out[step] = kept
            far_copies.append(
                send(
                    far_out.at[step],
                    far_in.at[step],
                    far_send.at[step],
                    far_recv.at[step],
                    {"width": 2 * lax.rem(chip + 1 + step, outer) + side},
                )
            )
        else:
            teach = kept

    def totals(filled):
        highest = jnp.max(filled, axis=1, keepdims=True)
        summed = jnp.sum(jnp.exp(filled - highest), axis=1, keepdims=True)
        return to_row(highest), to_row(summed)

    sq_own.wait()
    for copy in sq_copies:
        copy.wait_recv()
    sp_copy.wait()
    queries_all = sq_all[...].reshape(queries, s_width)
    learn = lax.dot_general(queries_all, sp_v[...], NT, preferred_element_type=jnp.float32)
    learn_fill = jnp.where(masked, MASK_FILL, learn * s_scale)
    learn_high, learn_sum = totals(learn_fill)

    for step, copy in enumerate(far_copies):
        copy.wait_recv()
        teach = teach + far_in[step]
    teach_fill = jnp.where(masked, MASK_FILL, teach * t_scale)
    teach_high, teach_sum = totals(teach_fill)

    def write(ref, values):
        for i, value in enumerate(values):
            ref[i : i + 1, :queries] = value

    def combine(ref, count):
        merged = []
        for place in (0, 2):
            highs = [ref[i][place : place + 1, :queries] for i in range(count)]
            sums = [ref[i][place + 1 : place + 2, :queries] for i in range(count)]
            high = functools.reduce(jnp.maximum, highs)
            total = functools.reduce(
                jnp.add, [s * jnp.exp(h - high) for h, s in zip(highs, sums)]
            )
            merged += [high, total]
        return merged

    def exchange(ref, axis, count, me, send_sems, recv_sems):
        copies = []
        for k in range(1, count):
            copies.append(
                send(
                    ref.at[0],
                    ref.at[k],
                    send_sems.at[k],
                    recv_sems.at[k],
                    {axis: lax.rem(me + k, count)},
                )
            )
        for copy in copies:
            copy.wait_recv()

    stat_w[0] = jnp.zeros(stat_w.shape[1:], jnp.float32)
    stat_b[0] = jnp.zeros(stat_b.shape[1:], jnp.float32)
    write(stat_w.at[0], (teach_high, teach_sum, learn_high, learn_sum))
    exchange(stat_w, "width", widths, w, statw_send, statw_recv)
    write(stat_b.at[0], combine(stat_w, widths))
    exchange(stat_b, "blk", blocks, b, statb_send, statb_recv)
    teach_high, teach_sum, learn_high, learn_sum = combine(stat_b, blocks)
    teach_log = to_column(teach_high + jnp.log(teach_sum))
    learn_log = to_column(learn_high + jnp.log(learn_sum))
    teach_probs = jnp.exp(teach_fill - teach_log)
    learn_probs = jnp.exp(learn_fill - learn_log)
    slope = (2.0 * learn_probs - teach_probs - is_positive.astype(jnp.float32)).astype(
        jnp.bfloat16
    )

    grad = jnp.dot(slope, sp_v[...], preferred_element_type=jnp.float32) * s_scale
    rows = panel // 2
    cols = s_width // outer
    for place in range(widths):
        half, col = place % 2, place // 2
        for block in range(blocks):
            top = block * panel + half * rows
            piece_out[place, block] = grad[top : top + rows, col * cols : (col + 1) * cols]
    piece_copies = []
    for k in range(1, widths):
        to = lax.rem(w + k, widths)
        piece_copies.append(
            send(
                piece_out.at[to],
                piece_in.at[k],
                piece_send.at[k],
                piece_recv.at[k],
                {"width": to},
            )
        )

    tall = min(own, 128)
    gp_copies = []

    def passage_part(i):
        part = lax.dot_general(
            slope[:, i * tall : (i + 1) * tall],
            queries_all,
            TN,
            preferred_element_type=jnp.float32,
        )
        gp_v[i * tall : (i + 1) * tall, :] = part * s_scale
        copy = pltpu.make_async_copy(
            gp_v.at[i * tall : (i + 1) * tall, :],
            gp_ref.at[i * tall : (i + 1) * tall, :],
            local_sem.at[5 + widths + i],
        )
        copy.start()
        gp_copies.append(copy)

    parts = own // tall
    for i in range(parts // 2):
        passage_part(i)

    total = piece_out[w]
    for k, copy in enumerate(piece_copies):
        copy.wait_recv()
        total = total + piece_in[k + 1]
    block_out[...] = total
    block_copies = []
    for k in range(1, blocks):
        to = lax.rem(b + k, blocks)
        block_copies.append(
            send(
                block_out.at[to],
                block_in.at[k],
                block_send.at[k],
                block_recv.at[k],
                {"blk": to},
            )
        )
    for i in range(parts // 2, parts):
        passage_part(i)
    total = block_out[b]
    for k, copy in enumerate(block_copies):
        copy.wait_recv()
        total = total + block_in[k + 1]
    final_in[w] = total
    final_copies = []
    for k in range(1, widths):
        final_copies.append(
            send(
                final_in.at[w],
                final_in.at[w],
                final_send.at[k],
                final_recv.at[k],
                {"width": lax.rem(w + k, widths)},
            )
        )
    for copy in final_copies:
        copy.wait_recv()
    for place in range(widths):
        half, col = place % 2, place // 2
        gq_ref[half * rows : (half + 1) * rows, col * cols : (col + 1) * cols] = final_in[place]

    for copy in gp_copies:
        copy.wait()
    for copy in pending:
        copy.wait_send()


def solution(mesh):
    blocks, widths = mesh.shape["blk"], mesh.shape["width"]

    def body(t_query, t_pass, s_query, s_pass, positive, doc_ids):
        panel, s_width = s_query.shape
        own = s_pass.shape[0]
        feats = t_query.shape[1]
        queries = blocks * panel
        outer = widths // 2
        rows, cols = panel // 2, s_width // outer
        f32, bf16 = jnp.float32, jnp.bfloat16
        lines = doc_ids.shape[0] // LANES
        dma = pltpu.SemaphoreType.DMA
        any_space = pl.BlockSpec(memory_space=pl.ANY)
        far = max(outer - 1, 1)
        stat_lanes = max(queries, LANES)
        return pl.pallas_call(
            functools.partial(kernel, (blocks, widths, feats * widths, s_width)),
            out_shape=(
                jax.ShapeDtypeStruct((panel, s_width), f32),
                jax.ShapeDtypeStruct((own, s_width), f32),
            ),
            in_specs=[any_space] * 6,
            out_specs=(pl.BlockSpec(memory_space=pltpu.VMEM), any_space),
            scratch_shapes=[
                pltpu.VMEM((blocks, panel, feats), bf16),
                pltpu.VMEM((widths, own, feats), bf16),
                pltpu.VMEM((blocks, panel, s_width), bf16),
                pltpu.VMEM((own, s_width), bf16),
                pltpu.VMEM((1, queries), jnp.int32),
                pltpu.VMEM((lines, LANES), jnp.int32),
                pltpu.VMEM((outer, queries, own), f32),
                pltpu.VMEM((outer, queries, own), f32),
                pltpu.VMEM((far, queries, own), f32),
                pltpu.VMEM((far, queries, own), f32),
                pltpu.VMEM((widths, 8, stat_lanes), f32),
                pltpu.VMEM((blocks, 8, stat_lanes), f32),
                pltpu.VMEM((widths, blocks, rows, cols), f32),
                pltpu.VMEM((widths, blocks, rows, cols), f32),
                pltpu.VMEM((blocks, rows, cols), f32),
                pltpu.VMEM((blocks, rows, cols), f32),
                pltpu.VMEM((widths, rows, cols), f32),
                pltpu.VMEM((own, s_width), f32),
                dma((5 + widths + own // LANES,)),
                dma((blocks,)),
                dma((blocks,)),
                dma((blocks,)),
                dma((blocks,)),
                dma((outer,)),
                dma((outer,)),
                dma((far,)),
                dma((far,)),
                dma((widths,)),
                dma((widths,)),
                dma((blocks,)),
                dma((blocks,)),
                dma((widths,)),
                dma((widths,)),
                dma((blocks,)),
                dma((blocks,)),
                dma((widths,)),
                dma((widths,)),
            ],
            compiler_params=pltpu.CompilerParams(
                collective_id=0, has_side_effects=True, vmem_limit_bytes=40 * 1024 * 1024
            ),
        )(
            t_query,
            t_pass,
            s_query,
            s_pass,
            positive.reshape(1, queries),
            doc_ids.reshape(lines, LANES),
        )

    placed = (
        P(("groups", "blk"), "width"),
        P(("groups", "blk"), "width"),
        P(("groups", "blk"), None),
        P(("groups", "blk", "width"), None),
        P("groups"),
        P("groups"),
    )
    return jax.shard_map(
        body,
        mesh=mesh,
        in_specs=placed,
        out_specs=(P(("groups", "blk"), None), P(("groups", "blk", "width"), None)),
        check_vma=False,
    )
```

```python
import functools
import math

import jax
import jax.numpy as jnp
from jax import lax
from jax.experimental import pallas as pl
from jax.experimental.pallas import tpu as pltpu
from jax.sharding import PartitionSpec as P

TEMPER = 2.0
MASK_FILL = -1e30
LANES = 128
MESH_ID = pl.DeviceIdType.MESH
NT = (((1,), (1,)), ((), ()))
TN = (((0,), (0,)), ((), ()))


def kernel(
    sizes,
    tq_ref,
    tp_ref,
    sq_ref,
    sp_ref,
    pos_ref,
    doc_ref,
    gq_ref,
    slope_ref,
    queries_ref,
    tq_all,
    tp_v,
    sq_all,
    sp_v,
    pos_v,
    doc_v,
    mate_out,
    mate_in,
    far_out,
    far_in,
    stat,
    piece_out,
    piece_in,
    final_in,
    slope_v,
    local_sem,
    tq_send,
    tq_recv,
    sq_send,
    sq_recv,
    mate_send,
    mate_recv,
    far_send,
    far_recv,
    stat_send,
    stat_recv,
    piece_send,
    piece_recv,
    final_send,
    final_recv,
):
    blocks, widths, t_width, s_width = sizes
    panel = sq_ref.shape[0]
    queries = blocks * panel
    own = sp_ref.shape[0]
    outer = widths // 2
    t_scale = TEMPER / math.sqrt(t_width)
    s_scale = TEMPER / math.sqrt(s_width)
    b = lax.axis_index("blk")
    w = lax.axis_index("width")
    side = lax.rem(w, 2)
    chip = w // 2
    pending = []

    group = blocks * widths
    me = b * widths + w

    def peer(k):
        other = lax.rem(me + k, group)
        return other, {"blk": other // widths, "width": lax.rem(other, widths)}

    def over(first, last, step, carry):
        if last - first < 16:
            for k in range(first, last):
                carry = step(k, carry)
            return carry
        return lax.fori_loop(first, last, step, carry)

    def each(step):
        def run(k, carry):
            step(k)
            return carry

        over(1, group, run, 0)

    barrier = pltpu.get_barrier_semaphore()
    each(
        lambda k: pl.semaphore_signal(
            barrier, inc=1, device_id=peer(k)[1], device_id_type=MESH_ID
        )
    )

    tq_own = pltpu.make_async_copy(tq_ref, tq_all.at[b], local_sem.at[0])
    sq_own = pltpu.make_async_copy(sq_ref, sq_all.at[b], local_sem.at[1])
    sp_copy = pltpu.make_async_copy(sp_ref, sp_v, local_sem.at[2])
    pos_copy = pltpu.make_async_copy(pos_ref, pos_v, local_sem.at[3])
    doc_copy = pltpu.make_async_copy(doc_ref, doc_v, local_sem.at[4])
    tq_own.start()
    sq_own.start()
    pos_copy.start()
    doc_copy.start()
    tp_copies = []
    for step in range(outer):
        target = lax.rem(chip + 1 + step, outer)
        for part in range(2):
            place = 2 * target + (1 - side if part == 0 else side)
            slot = 2 * step + part
            copy = pltpu.make_async_copy(
                tp_ref.at[pl.ds(pl.multiple_of(place * own, own), own), :],
                tp_v.at[slot],
                local_sem.at[5 + slot],
            )
            copy.start()
            tp_copies.append(copy)
    sp_copy.start()

    pl.semaphore_wait(barrier, group - 1)

    def send(src, dst, send_sem, recv_sem, where):
        copy = pltpu.make_async_remote_copy(
            src_ref=src,
            dst_ref=dst,
            send_sem=send_sem,
            recv_sem=recv_sem,
            device_id=where,
            device_id_type=MESH_ID,
        )
        copy.start()
        pending.append(copy)
        return copy

    tq_copies, sq_copies = [], []
    for k in range(1, blocks):
        to = {"blk": lax.rem(b + k, blocks)}
        tq_copies.append(send(tq_ref, tq_all.at[b], tq_send.at[k], tq_recv.at[k], to))

    eye = lax.broadcasted_iota(jnp.int32, (queries, queries), 0) == lax.broadcasted_iota(
        jnp.int32, (queries, queries), 1
    )

    def to_row(column):
        return jnp.sum(jnp.where(eye, column, 0.0), axis=0, keepdims=True)

    def to_column(row):
        return jnp.sum(jnp.where(eye, row, 0.0), axis=1, keepdims=True)

    pos_copy.wait()
    doc_copy.wait()
    positive = to_column(pos_v[...].astype(jnp.float32)).astype(jnp.int32)
    lane = lax.broadcasted_iota(jnp.int32, (1, LANES), 1)

    def look(row, found):
        docs = doc_v[pl.ds(row, 1), :]
        return jnp.where(positive - row * LANES == lane, docs, found)

    found = lax.fori_loop(
        0, doc_v.shape[0], look, jnp.full((queries, LANES), -1, jnp.int32), unroll=4
    )
    target_docs = jnp.max(found.astype(jnp.float32), axis=1, keepdims=True).astype(jnp.int32)
    first_row = (b * widths + w) * own
    first_line = (b * widths + w) * (own // LANES)
    docs = jnp.concatenate(
        [doc_v[pl.ds(first_line + j, 1), :] for j in range(own // LANES)], axis=1
    )
    columns = first_row + lax.broadcasted_iota(jnp.int32, (1, own), 1)
    is_positive = columns == positive
    masked = (docs == target_docs) & jnp.logical_not(is_positive)

    tq_own.wait()
    for copy in tq_copies:
        copy.wait_recv()
    for k in range(1, blocks):
        to = {"blk": lax.rem(b + k, blocks)}
        sq_copies.append(send(sq_ref, sq_all.at[b], sq_send.at[k], sq_recv.at[k], to))
    panels = tq_all[...].reshape(queries, tq_all.shape[2])

    def partial_scores(slot):
        tp_copies[slot].wait()
        return lax.dot_general(panels, tp_v[slot], NT, preferred_element_type=jnp.float32)

    teach = None
    far_copies = []
    for step in range(outer):
        mate_out[step] = partial_scores(2 * step)
        mate_copy = send(
            mate_out.at[step],
            mate_in.at[step],
            mate_send.at[step],
            mate_recv.at[step],
            {"width": w + 1 - 2 * side},
        )
        kept = partial_scores(2 * step + 1)
        mate_copy.wait_recv()
        kept = kept + mate_in[step]
        if step < outer - 1:
            far_out[step] = kept
            far_copies.append(
                send(
                    far_out.at[step],
                    far_in.at[step],
                    far_send.at[step],
                    far_recv.at[step],
                    {"width": 2 * lax.rem(chip + 1 + step, outer) + side},
                )
            )
        else:
            teach = kept

    def totals(filled):
        highest = jnp.max(filled, axis=1, keepdims=True)
        summed = jnp.sum(jnp.exp(filled - highest), axis=1, keepdims=True)
        return to_row(highest), to_row(summed)

    sq_own.wait()
    for copy in sq_copies:
        copy.wait_recv()
    sp_copy.wait()
    queries_all = sq_all[...].reshape(queries, s_width)
    learn = lax.dot_general(queries_all, sp_v[...], NT, preferred_element_type=jnp.float32)
    learn_fill = jnp.where(masked, MASK_FILL, learn * s_scale)
    learn_high, learn_sum = totals(learn_fill)

    for step, copy in enumerate(far_copies):
        copy.wait_recv()
        teach = teach + far_in[step]
    teach_fill = jnp.where(masked, MASK_FILL, teach * t_scale)
    teach_high, teach_sum = totals(teach_fill)

    for i, value in enumerate((teach_high, learn_high, teach_sum, learn_sum)):
        stat[0, i : i + 1, :queries] = value

    def stat_copy(k):
        return pltpu.make_async_remote_copy(
            src_ref=stat.at[0],
            dst_ref=stat.at[k],
            send_sem=stat_send.at[k],
            recv_sem=stat_recv.at[k],
            device_id=peer(k)[1],
            device_id_type=MESH_ID,
        )

    each(lambda k: stat_copy(k).start())
    each(lambda k: stat_copy(k).wait_recv())

    def highs(k):
        return stat[k, 0:2, :queries]

    high = over(1, group, lambda k, best: jnp.maximum(best, highs(k)), highs(0))

    def add_total(k, total):
        return total + stat[k, 2:4, :queries] * jnp.exp(highs(k) - high)

    logs = high + jnp.log(over(0, group, add_total, jnp.zeros((2, queries), jnp.float32)))
    teach_log = to_column(logs[0:1])
    learn_log = to_column(logs[1:2])
    teach_probs = jnp.exp(teach_fill - teach_log)
    learn_probs = jnp.exp(learn_fill - learn_log)
    slope = (2.0 * learn_probs - teach_probs - is_positive.astype(jnp.float32)).astype(
        jnp.bfloat16
    )

    grad = jnp.dot(slope, sp_v[...], preferred_element_type=jnp.float32) * s_scale
    rows = panel // 2
    cols = s_width // outer
    for block in range(blocks):
        for place in range(widths):
            half, col = place % 2, place // 2
            top = block * panel + half * rows
            piece_out[block * widths + place] = grad[
                top : top + rows, col * cols : (col + 1) * cols
            ]

    def piece_copy(k):
        other, to = peer(k)
        return pltpu.make_async_remote_copy(
            src_ref=piece_out.at[other],
            dst_ref=piece_in.at[k],
            send_sem=piece_send.at[k],
            recv_sem=piece_recv.at[k],
            device_id=to,
            device_id_type=MESH_ID,
        )

    each(lambda k: piece_copy(k).start())

    slope_v[...] = slope
    slope_copy = pltpu.make_async_copy(slope_v, slope_ref, local_sem.at[5 + widths])
    queries_copy = pltpu.make_async_copy(sq_all, queries_ref, local_sem.at[6 + widths])
    slope_copy.start()
    queries_copy.start()

    each(lambda k: piece_copy(k).wait_recv())
    total = over(1, group, lambda k, total: total + piece_in[k], piece_out[me])
    final_in[w] = total
    final_copies = []
    for k in range(1, widths):
        final_copies.append(
            send(
                final_in.at[w],
                final_in.at[w],
                final_send.at[k],
                final_recv.at[k],
                {"width": lax.rem(w + k, widths)},
            )
        )
    for copy in final_copies:
        copy.wait_recv()
    for place in range(widths):
        half, col = place % 2, place // 2
        gq_ref[half * rows : (half + 1) * rows, col * cols : (col + 1) * cols] = final_in[place]

    slope_copy.wait()
    queries_copy.wait()
    for copy in pending:
        copy.wait_send()
    each(lambda k: stat_copy(k).wait_send())
    each(lambda k: piece_copy(k).wait_send())


def solution(mesh):
    blocks, widths = mesh.shape["blk"], mesh.shape["width"]

    def body(t_query, t_pass, s_query, s_pass, positive, doc_ids):
        panel, s_width = s_query.shape
        own = s_pass.shape[0]
        feats = t_query.shape[1]
        queries = blocks * panel
        outer = widths // 2
        rows, cols = panel // 2, s_width // outer
        group = blocks * widths
        f32, bf16 = jnp.float32, jnp.bfloat16
        lines = doc_ids.shape[0] // LANES
        dma = pltpu.SemaphoreType.DMA
        any_space = pl.BlockSpec(memory_space=pltpu.HBM)
        far = max(outer - 1, 1)
        stat_lanes = max(queries, LANES)
        vmem_space = pl.BlockSpec(memory_space=pltpu.VMEM)
        grad_query, slope, queries_all = pl.pallas_call(
            functools.partial(kernel, (blocks, widths, feats * widths, s_width)),
            out_shape=(
                jax.ShapeDtypeStruct((panel, s_width), f32),
                jax.ShapeDtypeStruct((queries, own), bf16),
                jax.ShapeDtypeStruct((blocks, panel, s_width), bf16),
            ),
            in_specs=[any_space] * 6,
            out_specs=(vmem_space, any_space, any_space),
            scratch_shapes=[
                pltpu.VMEM((blocks, panel, feats), bf16),
                pltpu.VMEM((widths, own, feats), bf16),
                pltpu.VMEM((blocks, panel, s_width), bf16),
                pltpu.VMEM((own, s_width), bf16),
                pltpu.VMEM((1, queries), jnp.int32),
                pltpu.VMEM((lines, LANES), jnp.int32),
                pltpu.VMEM((outer, queries, own), f32),
                pltpu.VMEM((outer, queries, own), f32),
                pltpu.VMEM((far, queries, own), f32),
                pltpu.VMEM((far, queries, own), f32),
                pltpu.VMEM((group, 4, stat_lanes), f32),
                pltpu.VMEM((group, rows, cols), f32),
                pltpu.VMEM((group, rows, cols), f32),
                pltpu.VMEM((widths, rows, cols), f32),
                pltpu.VMEM((queries, own), bf16),
                dma((7 + widths,)),
                dma((blocks,)),
                dma((blocks,)),
                dma((blocks,)),
                dma((blocks,)),
                dma((outer,)),
                dma((outer,)),
                dma((far,)),
                dma((far,)),
                dma((group,)),
                dma((group,)),
                dma((group,)),
                dma((group,)),
                dma((widths,)),
                dma((widths,)),
            ],
            compiler_params=pltpu.CompilerParams(
                collective_id=0, has_side_effects=True, vmem_limit_bytes=60 * 1024 * 1024
            ),
        )(
            t_query,
            t_pass,
            s_query,
            s_pass,
            positive.reshape(1, queries),
            doc_ids.reshape(lines, LANES),
        )
        s_scale = TEMPER / math.sqrt(s_width)
        grad_passage = s_scale * lax.dot_general(
            slope, queries_all.reshape(queries, s_width), TN, preferred_element_type=f32
        )
        return grad_query, grad_passage

    placed = (
        P(("groups", "blk"), "width"),
        P(("groups", "blk"), "width"),
        P(("groups", "blk"), None),
        P(("groups", "blk", "width"), None),
        P("groups"),
        P("groups"),
    )
    return jax.shard_map(
        body,
        mesh=mesh,
        in_specs=placed,
        out_specs=(P(("groups", "blk"), None), P(("groups", "blk", "width"), None)),
        check_vma=False,
    )
```

```python
import functools
import math

import jax
import jax.numpy as jnp
from jax import lax
from jax.experimental import pallas as pl
from jax.experimental.pallas import tpu as pltpu
from jax.sharding import PartitionSpec as P

TEMPER = 2.0
MASK_FILL = -1e30
LANES = 128
MESH_ID = pl.DeviceIdType.MESH
NT = (((1,), (1,)), ((), ()))
TN = (((0,), (0,)), ((), ()))


def kernel(
    sizes,
    tq_ref,
    tp_ref,
    sq_ref,
    sp_ref,
    pos_ref,
    doc_ref,
    gq_ref,
    slope_ref,
    queries_ref,
    tq_all,
    tp_v,
    sq_all,
    sp_v,
    pos_v,
    doc_v,
    mate_out,
    mate_in,
    far_out,
    far_in,
    stat,
    piece_out,
    piece_in,
    final,
    slope_v,
    local_sem,
    tq_send,
    tq_recv,
    sq_send,
    sq_recv,
    mate_send,
    mate_recv,
    far_send,
    far_recv,
    stat_send,
    stat_recv,
    piece_send,
    piece_recv,
    final_send,
    final_recv,
):
    blocks, widths, t_width, s_width = sizes
    panel = sq_ref.shape[0]
    queries = blocks * panel
    own = sp_ref.shape[0]
    outer = widths // 2
    t_scale = TEMPER / math.sqrt(t_width)
    s_scale = TEMPER / math.sqrt(s_width)
    b = lax.axis_index("blk")
    w = lax.axis_index("width")
    side = lax.rem(w, 2)
    chip = w // 2
    pending = []

    group = blocks * widths
    me = b * widths + w

    def peer(k):
        other = lax.rem(me + k, group)
        return other, {"blk": other // widths, "width": lax.rem(other, widths)}

    def over(first, last, step, carry):
        if last - first < 16:
            for k in range(first, last):
                carry = step(k, carry)
            return carry
        return lax.fori_loop(first, last, step, carry)

    def each(step):
        def run(k, carry):
            step(k)
            return carry

        over(1, group, run, 0)

    barrier = pltpu.get_barrier_semaphore()
    each(
        lambda k: pl.semaphore_signal(
            barrier, inc=1, device_id=peer(k)[1], device_id_type=MESH_ID
        )
    )

    tq_own = pltpu.make_async_copy(tq_ref, tq_all.at[b], local_sem.at[0])
    sq_own = pltpu.make_async_copy(sq_ref, sq_all.at[b], local_sem.at[1])
    sp_copy = pltpu.make_async_copy(sp_ref, sp_v, local_sem.at[2])
    pos_copy = pltpu.make_async_copy(pos_ref, pos_v, local_sem.at[3])
    doc_copy = pltpu.make_async_copy(doc_ref, doc_v, local_sem.at[4])
    tq_own.start()
    sq_own.start()
    pos_copy.start()
    doc_copy.start()
    tp_copies = []
    for step in range(outer):
        target = lax.rem(chip + 1 + step, outer)
        for part in range(2):
            place = 2 * target + (1 - side if part == 0 else side)
            slot = 2 * step + part
            copy = pltpu.make_async_copy(
                tp_ref.at[pl.ds(pl.multiple_of(place * own, own), own), :],
                tp_v.at[slot],
                local_sem.at[5 + slot],
            )
            copy.start()
            tp_copies.append(copy)
    sp_copy.start()

    pl.semaphore_wait(barrier, group - 1)

    def send(src, dst, send_sem, recv_sem, where):
        copy = pltpu.make_async_remote_copy(
            src_ref=src,
            dst_ref=dst,
            send_sem=send_sem,
            recv_sem=recv_sem,
            device_id=where,
            device_id_type=MESH_ID,
        )
        copy.start()
        pending.append(copy)
        return copy

    tq_copies, sq_copies = [], []
    for k in range(1, blocks):
        to = {"blk": lax.rem(b + k, blocks)}
        tq_copies.append(send(tq_ref, tq_all.at[b], tq_send.at[k], tq_recv.at[k], to))

    eye = lax.broadcasted_iota(jnp.int32, (queries, queries), 0) == lax.broadcasted_iota(
        jnp.int32, (queries, queries), 1
    )

    def to_row(column):
        return jnp.sum(jnp.where(eye, column, 0.0), axis=0, keepdims=True)

    def to_column(row):
        return jnp.sum(jnp.where(eye, row, 0.0), axis=1, keepdims=True)

    pos_copy.wait()
    doc_copy.wait()
    positive = to_column(pos_v[...].astype(jnp.float32)).astype(jnp.int32)
    lane = lax.broadcasted_iota(jnp.int32, (1, LANES), 1)

    def look(row, found):
        docs = doc_v[pl.ds(row, 1), :]
        return jnp.where(positive - row * LANES == lane, docs, found)

    found = lax.fori_loop(
        0, doc_v.shape[0], look, jnp.full((queries, LANES), -1, jnp.int32), unroll=4
    )
    target_docs = jnp.max(found.astype(jnp.float32), axis=1, keepdims=True).astype(jnp.int32)
    first_row = (b * widths + w) * own
    first_line = (b * widths + w) * (own // LANES)
    docs = jnp.concatenate(
        [doc_v[pl.ds(first_line + j, 1), :] for j in range(own // LANES)], axis=1
    )
    columns = first_row + lax.broadcasted_iota(jnp.int32, (1, own), 1)
    is_positive = columns == positive
    masked = (docs == target_docs) & jnp.logical_not(is_positive)

    tq_own.wait()
    for copy in tq_copies:
        copy.wait_recv()
    for k in range(1, blocks):
        to = {"blk": lax.rem(b + k, blocks)}
        sq_copies.append(send(sq_ref, sq_all.at[b], sq_send.at[k], sq_recv.at[k], to))
    panels = tq_all[...].reshape(queries, tq_all.shape[2])

    wide = own // 2
    loaded = set()

    def partial_scores(slot, half):
        if slot not in loaded:
            loaded.add(slot)
            tp_copies[slot].wait()
        part = tp_v[slot, half * wide : (half + 1) * wide, :]
        return lax.dot_general(panels, part, NT, preferred_element_type=jnp.float32)

    mate_copies, far_copies, kept = [], [], []

    def finish(half, step):
        place = 2 * step + half
        mate_copies[place].wait_recv()
        summed = kept[place] + mate_in[place]
        if step == outer - 1:
            return summed
        far_out[place] = summed
        far_copies.append(
            send(
                far_out.at[place],
                far_in.at[place],
                far_send.at[place],
                far_recv.at[place],
                {"width": 2 * lax.rem(chip + 1 + step, outer) + side},
            )
        )

    for step in range(outer):
        for half in range(2):
            place = 2 * step + half
            mate_out[place] = partial_scores(2 * step, half)
            mate_copies.append(
                send(
                    mate_out.at[place],
                    mate_in.at[place],
                    mate_send.at[place],
                    mate_recv.at[place],
                    {"width": w + 1 - 2 * side},
                )
            )
        if step > 0:
            finish(0, step - 1)
            finish(1, step - 1)
        for half in range(2):
            kept.append(partial_scores(2 * step + 1, half))

    def totals(filled):
        highest = jnp.max(filled, axis=1, keepdims=True)
        powers = jnp.exp(filled - highest)
        summed = jnp.sum(powers, axis=1, keepdims=True)
        return to_row(highest), to_row(summed)

    sq_own.wait()
    for copy in sq_copies:
        copy.wait_recv()
    sp_copy.wait()
    queries_all = sq_all[...].reshape(queries, s_width)
    learn = lax.dot_general(queries_all, sp_v[...], NT, preferred_element_type=jnp.float32)
    learn_fill = jnp.where(masked, MASK_FILL, learn * s_scale)
    learn_high, learn_sum = totals(learn_fill)

    teach = [finish(half, outer - 1) for half in range(2)]
    for place, copy in enumerate(far_copies):
        copy.wait_recv()
        teach[place % 2] = teach[place % 2] + far_in[place]
    teach = jnp.concatenate(teach, axis=1)
    teach_fill = jnp.where(masked, MASK_FILL, teach * t_scale)
    teach_high, teach_sum = totals(teach_fill)

    for i, value in enumerate((teach_high, learn_high, teach_sum, learn_sum)):
        stat[0, i : i + 1, :queries] = value

    def wait_all(ref, sem):
        whole = ref.at[pl.ds(1, group - 1)]
        pltpu.make_async_copy(whole, whole, sem).wait()

    def stat_copy(k):
        return pltpu.make_async_remote_copy(
            src_ref=stat.at[0],
            dst_ref=stat.at[k],
            send_sem=stat_send.at[0],
            recv_sem=stat_recv.at[0],
            device_id=peer(k)[1],
            device_id_type=MESH_ID,
        )

    each(lambda k: stat_copy(k).start())
    wait_all(stat, stat_recv.at[0])

    def highs(k):
        return stat[k, 0:2, :queries]

    high = over(1, group, lambda k, best: jnp.maximum(best, highs(k)), highs(0))

    def add_total(k, total):
        return total + stat[k, 2:4, :queries] * jnp.exp(highs(k) - high)

    logs = high + jnp.log(over(0, group, add_total, jnp.zeros((2, queries), jnp.float32)))
    teach_log = to_column(logs[0:1])
    learn_log = to_column(logs[1:2])
    teach_probs = jnp.exp(teach_fill - teach_log)
    learn_probs = jnp.exp(learn_fill - learn_log)
    slope = (2.0 * learn_probs - teach_probs - is_positive.astype(jnp.float32)).astype(
        jnp.bfloat16
    )

    grad = jnp.dot(slope, sp_v[...], preferred_element_type=jnp.float32) * s_scale
    rows = panel // 2
    cols = s_width // outer
    for block in range(blocks):
        for place in range(widths):
            half, col = place % 2, place // 2
            top = block * panel + half * rows
            piece_out[block * widths + place] = grad[
                top : top + rows, col * cols : (col + 1) * cols
            ]

    def piece_copy(k):
        other, to = peer(k)
        return pltpu.make_async_remote_copy(
            src_ref=piece_out.at[other],
            dst_ref=piece_in.at[k],
            send_sem=piece_send.at[0],
            recv_sem=piece_recv.at[0],
            device_id=to,
            device_id_type=MESH_ID,
        )

    each(lambda k: piece_copy(k).start())

    slope_v[...] = slope
    slope_copy = pltpu.make_async_copy(slope_v, slope_ref, local_sem.at[5 + widths])
    queries_copy = pltpu.make_async_copy(sq_all, queries_ref, local_sem.at[6 + widths])
    slope_copy.start()
    queries_copy.start()

    wait_all(stat, stat_send.at[0])
    for copy in pending:
        copy.wait_send()
    slope_copy.wait()
    queries_copy.wait()
    pending.clear()
    wait_all(piece_in, piece_recv.at[0])
    total = over(1, group, lambda k, total: total + piece_in[k], piece_out[me])
    final[...] = total
    if len(gq_ref.shape) == 3:
        place = gq_ref.at[w]
    else:
        place = gq_ref.at[
            pl.ds(pl.multiple_of(side * rows, rows), rows),
            pl.ds(pl.multiple_of(chip * cols, cols), cols),
        ]
    final_own = pltpu.make_async_copy(final, place, local_sem.at[0])
    final_own.start()
    final_copies = []
    for k in range(1, widths):
        final_copies.append(
            send(
                final,
                place,
                final_send.at[k],
                final_recv.at[k],
                {"width": lax.rem(w + k, widths)},
            )
        )
    wait_all(piece_in, piece_send.at[0])
    final_own.wait()
    for copy in final_copies:
        copy.wait_recv()
    for copy in pending:
        copy.wait_send()


def solution(mesh):
    blocks, widths = mesh.shape["blk"], mesh.shape["width"]

    def body(t_query, t_pass, s_query, s_pass, positive, doc_ids):
        panel, s_width = s_query.shape
        own = s_pass.shape[0]
        feats = t_query.shape[1]
        queries = blocks * panel
        outer = widths // 2
        rows, cols = panel // 2, s_width // outer
        whole_tiles = rows % 8 == 0 and cols % LANES == 0
        gq_shape = (panel, s_width) if whole_tiles else (widths, rows, cols)
        group = blocks * widths
        f32, bf16 = jnp.float32, jnp.bfloat16
        lines = doc_ids.shape[0] // LANES
        dma = pltpu.SemaphoreType.DMA
        any_space = pl.BlockSpec(memory_space=pltpu.HBM)
        far = max(outer - 1, 1)
        stat_lanes = max(queries, LANES)
        grad_query, slope, queries_all = pl.pallas_call(
            functools.partial(kernel, (blocks, widths, feats * widths, s_width)),
            out_shape=(
                jax.ShapeDtypeStruct(gq_shape, f32),
                jax.ShapeDtypeStruct((queries, own), bf16),
                jax.ShapeDtypeStruct((blocks, panel, s_width), bf16),
            ),
            in_specs=[any_space] * 6,
            out_specs=(any_space,) * 3,
            scratch_shapes=[
                pltpu.VMEM((blocks, panel, feats), bf16),
                pltpu.VMEM((widths, own, feats), bf16),
                pltpu.VMEM((blocks, panel, s_width), bf16),
                pltpu.VMEM((own, s_width), bf16),
                pltpu.VMEM((1, queries), jnp.int32),
                pltpu.VMEM((lines, LANES), jnp.int32),
                pltpu.VMEM((2 * outer, queries, own // 2), f32),
                pltpu.VMEM((2 * outer, queries, own // 2), f32),
                pltpu.VMEM((2 * far, queries, own // 2), f32),
                pltpu.VMEM((2 * far, queries, own // 2), f32),
                pltpu.VMEM((group, 4, stat_lanes), f32),
                pltpu.VMEM((group, rows, cols), f32),
                pltpu.VMEM((group, rows, cols), f32),
                pltpu.VMEM((rows, cols), f32),
                pltpu.VMEM((queries, own), bf16),
                dma((7 + widths,)),
                dma((blocks,)),
                dma((blocks,)),
                dma((blocks,)),
                dma((blocks,)),
                dma((2 * outer,)),
                dma((2 * outer,)),
                dma((2 * far,)),
                dma((2 * far,)),
                dma((1,)),
                dma((1,)),
                dma((1,)),
                dma((1,)),
                dma((widths,)),
                dma((widths,)),
            ],
            compiler_params=pltpu.CompilerParams(
                collective_id=0, has_side_effects=True, vmem_limit_bytes=60 * 1024 * 1024
            ),
        )(
            t_query,
            t_pass,
            s_query,
            s_pass,
            positive.reshape(1, queries),
            doc_ids.reshape(lines, LANES),
        )
        s_scale = TEMPER / math.sqrt(s_width)
        grad_passage = s_scale * lax.dot_general(
            slope, queries_all.reshape(queries, s_width), TN, preferred_element_type=f32
        )
        if not whole_tiles:
            pieces = grad_query.reshape(outer, 2, rows, cols)
            grad_query = pieces.transpose(1, 2, 0, 3).reshape(panel, s_width)
        return grad_query, grad_passage

    placed = (
        P(("groups", "blk"), "width"),
        P(("groups", "blk"), "width"),
        P(("groups", "blk"), None),
        P(("groups", "blk", "width"), None),
        P("groups"),
        P("groups"),
    )
    return jax.shard_map(
        body,
        mesh=mesh,
        in_specs=placed,
        out_specs=(P(("groups", "blk"), None), P(("groups", "blk", "width"), None)),
        check_vma=False,
    )
```

```python
import functools
import math

import jax
import jax.numpy as jnp
from jax import lax
from jax.experimental import pallas as pl
from jax.experimental.pallas import tpu as pltpu
from jax.sharding import PartitionSpec as P

TEMPER = 2.0
MASK_FILL = -1e30
LANES = 128
MESH_ID = pl.DeviceIdType.MESH
NT = (((1,), (1,)), ((), ()))
TN = (((0,), (0,)), ((), ()))


def kernel(
    sizes,
    tq_ref,
    tp_ref,
    sq_ref,
    sp_ref,
    pos_ref,
    doc_ref,
    gq_ref,
    slope_ref,
    queries_ref,
    tq_all,
    tp_v,
    sq_all,
    sp_v,
    pos_v,
    doc_v,
    mate_out,
    mate_in,
    far_out,
    far_in,
    stat,
    piece_out,
    piece_in,
    final,
    slope_v,
    local_sem,
    tq_send,
    tq_recv,
    sq_send,
    sq_recv,
    mate_send,
    mate_recv,
    far_send,
    far_recv,
    stat_send,
    stat_recv,
    piece_send,
    piece_recv,
    final_send,
    final_recv,
):
    blocks, widths, t_width, s_width = sizes
    panel = sq_ref.shape[0]
    queries = blocks * panel
    own = sp_ref.shape[0]
    outer = widths // 2
    t_scale = TEMPER / math.sqrt(t_width)
    s_scale = TEMPER / math.sqrt(s_width)
    b = lax.axis_index("blk")
    w = lax.axis_index("width")
    side = lax.rem(w, 2)
    chip = w // 2
    pending = []

    group = blocks * widths
    me = b * widths + w

    def peer(k):
        other = lax.rem(me + k, group)
        return other, {"blk": other // widths, "width": lax.rem(other, widths)}

    def over(first, last, step, carry):
        if last - first < 16:
            for k in range(first, last):
                carry = step(k, carry)
            return carry
        return lax.fori_loop(first, last, step, carry)

    def each(step):
        def run(k, carry):
            step(k)
            return carry

        over(1, group, run, 0)

    barrier = pltpu.get_barrier_semaphore()
    each(
        lambda k: pl.semaphore_signal(
            barrier, inc=1, device_id=peer(k)[1], device_id_type=MESH_ID
        )
    )

    tq_own = pltpu.make_async_copy(tq_ref, tq_all.at[b], local_sem.at[0])
    sq_own = pltpu.make_async_copy(sq_ref, sq_all.at[b], local_sem.at[1])
    sp_copy = pltpu.make_async_copy(sp_ref, sp_v, local_sem.at[2])
    pos_copy = pltpu.make_async_copy(pos_ref, pos_v, local_sem.at[3])
    doc_copy = pltpu.make_async_copy(doc_ref, doc_v, local_sem.at[4])
    tq_own.start()
    sq_own.start()
    pos_copy.start()
    doc_copy.start()
    tp_copies = []
    for step in range(outer):
        target = lax.rem(chip + 1 + step, outer)
        for part in range(2):
            place = 2 * target + (1 - side if part == 0 else side)
            slot = 2 * step + part
            copy = pltpu.make_async_copy(
                tp_ref.at[pl.ds(pl.multiple_of(place * own, own), own), :],
                tp_v.at[slot],
                local_sem.at[5 + slot],
            )
            copy.start()
            tp_copies.append(copy)
    sp_copy.start()

    pl.semaphore_wait(barrier, group - 1)

    def send(src, dst, send_sem, recv_sem, where):
        copy = pltpu.make_async_remote_copy(
            src_ref=src,
            dst_ref=dst,
            send_sem=send_sem,
            recv_sem=recv_sem,
            device_id=where,
            device_id_type=MESH_ID,
        )
        copy.start()
        pending.append(copy)
        return copy

    tq_copies, sq_copies = [], []
    for k in range(1, blocks):
        to = {"blk": lax.rem(b + k, blocks)}
        tq_copies.append(send(tq_ref, tq_all.at[b], tq_send.at[k], tq_recv.at[k], to))

    eye = lax.broadcasted_iota(jnp.int32, (queries, queries), 0) == lax.broadcasted_iota(
        jnp.int32, (queries, queries), 1
    )

    def to_row(column):
        return jnp.sum(jnp.where(eye, column, 0.0), axis=0, keepdims=True)

    def to_column(row):
        return jnp.sum(jnp.where(eye, row, 0.0), axis=1, keepdims=True)

    pos_copy.wait()
    doc_copy.wait()
    positive = to_column(pos_v[...].astype(jnp.float32)).astype(jnp.int32)
    lane = lax.broadcasted_iota(jnp.int32, (1, LANES), 1)

    def look(row, found):
        docs = doc_v[pl.ds(row, 1), :]
        return jnp.where(positive - row * LANES == lane, docs, found)

    found = lax.fori_loop(
        0, doc_v.shape[0], look, jnp.full((queries, LANES), -1, jnp.int32), unroll=4
    )
    target_docs = jnp.max(found.astype(jnp.float32), axis=1, keepdims=True).astype(jnp.int32)
    first_row = (b * widths + w) * own
    first_line = (b * widths + w) * (own // LANES)
    docs = jnp.concatenate(
        [doc_v[pl.ds(first_line + j, 1), :] for j in range(own // LANES)], axis=1
    )
    columns = first_row + lax.broadcasted_iota(jnp.int32, (1, own), 1)
    is_positive = columns == positive
    masked = (docs == target_docs) & jnp.logical_not(is_positive)

    tq_own.wait()
    for copy in tq_copies:
        copy.wait_recv()
    for k in range(1, blocks):
        to = {"blk": lax.rem(b + k, blocks)}
        sq_copies.append(send(sq_ref, sq_all.at[b], sq_send.at[k], sq_recv.at[k], to))
    panels = tq_all[...].reshape(queries, tq_all.shape[2])

    wide = own // 2
    loaded = set()

    def partial_scores(slot, half):
        if slot not in loaded:
            loaded.add(slot)
            tp_copies[slot].wait()
        part = tp_v[slot, half * wide : (half + 1) * wide, :]
        return lax.dot_general(panels, part, NT, preferred_element_type=jnp.float32)

    mate_copies, far_copies, kept = [], [], []

    def finish(half, step):
        place = 2 * step + half
        mate_copies[place].wait_recv()
        summed = kept[place] + mate_in[place]
        if step == outer - 1:
            return summed
        far_out[place] = summed
        far_copies.append(
            send(
                far_out.at[place],
                far_in.at[place],
                far_send.at[place],
                far_recv.at[place],
                {"width": 2 * lax.rem(chip + 1 + step, outer) + side},
            )
        )

    for step in range(outer):
        for half in range(2):
            place = 2 * step + half
            mate_out[place] = partial_scores(2 * step, half)
            mate_copies.append(
                send(
                    mate_out.at[place],
                    mate_in.at[place],
                    mate_send.at[place],
                    mate_recv.at[place],
                    {"width": w + 1 - 2 * side},
                )
            )
        if step > 0:
            finish(0, step - 1)
            finish(1, step - 1)
        for half in range(2):
            kept.append(partial_scores(2 * step + 1, half))

    def totals(filled):
        highest = jnp.max(filled, axis=1, keepdims=True)
        powers = jnp.exp(filled - highest)
        summed = jnp.sum(powers, axis=1, keepdims=True)
        return to_row(highest), to_row(summed), highest, powers

    sq_own.wait()
    for copy in sq_copies:
        copy.wait_recv()
    sp_copy.wait()
    queries_all = sq_all[...].reshape(queries, s_width)
    learn = lax.dot_general(queries_all, sp_v[...], NT, preferred_element_type=jnp.float32)
    learn_fill = jnp.where(masked, MASK_FILL, learn * s_scale)
    learn_high, learn_sum, learn_top, learn_powers = totals(learn_fill)

    teach = [finish(half, outer - 1) for half in range(2)]
    for place, copy in enumerate(far_copies):
        copy.wait_recv()
        teach[place % 2] = teach[place % 2] + far_in[place]
    teach = jnp.concatenate(teach, axis=1)
    teach_fill = jnp.where(masked, MASK_FILL, teach * t_scale)
    teach_high, teach_sum, teach_top, teach_powers = totals(teach_fill)

    for i, value in enumerate((teach_high, learn_high, teach_sum, learn_sum)):
        stat[0, i : i + 1, :queries] = value

    def wait_all(ref, sem):
        whole = ref.at[pl.ds(1, group - 1)]
        pltpu.make_async_copy(whole, whole, sem).wait()

    def stat_copy(k):
        return pltpu.make_async_remote_copy(
            src_ref=stat.at[0],
            dst_ref=stat.at[k],
            send_sem=stat_send.at[0],
            recv_sem=stat_recv.at[0],
            device_id=peer(k)[1],
            device_id_type=MESH_ID,
        )

    each(lambda k: stat_copy(k).start())
    wait_all(stat, stat_recv.at[0])

    def highs(k):
        return stat[k, 0:2, :queries]

    high = over(1, group, lambda k, best: jnp.maximum(best, highs(k)), highs(0))

    def add_total(k, total):
        return total + stat[k, 2:4, :queries] * jnp.exp(highs(k) - high)

    logs = high + jnp.log(over(0, group, add_total, jnp.zeros((2, queries), jnp.float32)))
    teach_log = to_column(logs[0:1])
    learn_log = to_column(logs[1:2])
    teach_probs = teach_powers * jnp.exp(teach_top - teach_log)
    learn_probs = learn_powers * jnp.exp(learn_top - learn_log)
    slope = (2.0 * learn_probs - teach_probs - is_positive.astype(jnp.float32)).astype(
        jnp.bfloat16
    )

    grad = jnp.dot(slope, sp_v[...], preferred_element_type=jnp.float32) * s_scale
    rows = panel // 2
    cols = s_width // outer
    for block in range(blocks):
        for place in range(widths):
            half, col = place % 2, place // 2
            top = block * panel + half * rows
            piece_out[block * widths + place] = grad[
                top : top + rows, col * cols : (col + 1) * cols
            ]

    def piece_copy(k):
        other, to = peer(k)
        return pltpu.make_async_remote_copy(
            src_ref=piece_out.at[other],
            dst_ref=piece_in.at[k],
            send_sem=piece_send.at[0],
            recv_sem=piece_recv.at[0],
            device_id=to,
            device_id_type=MESH_ID,
        )

    each(lambda k: piece_copy(k).start())

    slope_v[...] = slope
    slope_copy = pltpu.make_async_copy(slope_v, slope_ref, local_sem.at[5 + widths])
    queries_copy = pltpu.make_async_copy(sq_all, queries_ref, local_sem.at[6 + widths])
    slope_copy.start()
    queries_copy.start()

    wait_all(stat, stat_send.at[0])
    for copy in pending:
        copy.wait_send()
    slope_copy.wait()
    queries_copy.wait()
    pending.clear()
    wait_all(piece_in, piece_recv.at[0])
    total = over(1, group, lambda k, total: total + piece_in[k], piece_out[me])
    final[...] = total
    if len(gq_ref.shape) == 3:
        place = gq_ref.at[w]
    else:
        place = gq_ref.at[
            pl.ds(pl.multiple_of(side * rows, rows), rows),
            pl.ds(pl.multiple_of(chip * cols, cols), cols),
        ]
    final_own = pltpu.make_async_copy(final, place, local_sem.at[0])
    final_own.start()
    final_copies = []
    for k in range(1, widths):
        final_copies.append(
            send(
                final,
                place,
                final_send.at[k],
                final_recv.at[k],
                {"width": lax.rem(w + k, widths)},
            )
        )
    wait_all(piece_in, piece_send.at[0])
    final_own.wait()
    for copy in final_copies:
        copy.wait_recv()
    for copy in pending:
        copy.wait_send()


def solution(mesh):
    blocks, widths = mesh.shape["blk"], mesh.shape["width"]

    def body(t_query, t_pass, s_query, s_pass, positive, doc_ids):
        panel, s_width = s_query.shape
        own = s_pass.shape[0]
        feats = t_query.shape[1]
        queries = blocks * panel
        outer = widths // 2
        rows, cols = panel // 2, s_width // outer
        whole_tiles = rows % 8 == 0 and cols % LANES == 0
        gq_shape = (panel, s_width) if whole_tiles else (widths, rows, cols)
        group = blocks * widths
        f32, bf16 = jnp.float32, jnp.bfloat16
        lines = doc_ids.shape[0] // LANES
        dma = pltpu.SemaphoreType.DMA
        any_space = pl.BlockSpec(memory_space=pltpu.HBM)
        far = max(outer - 1, 1)
        stat_lanes = max(queries, LANES)
        grad_query, slope, queries_all = pl.pallas_call(
            functools.partial(kernel, (blocks, widths, feats * widths, s_width)),
            out_shape=(
                jax.ShapeDtypeStruct(gq_shape, f32),
                jax.ShapeDtypeStruct((queries, own), bf16),
                jax.ShapeDtypeStruct((blocks, panel, s_width), bf16),
            ),
            in_specs=[any_space] * 6,
            out_specs=(any_space,) * 3,
            scratch_shapes=[
                pltpu.VMEM((blocks, panel, feats), bf16),
                pltpu.VMEM((widths, own, feats), bf16),
                pltpu.VMEM((blocks, panel, s_width), bf16),
                pltpu.VMEM((own, s_width), bf16),
                pltpu.VMEM((1, queries), jnp.int32),
                pltpu.VMEM((lines, LANES), jnp.int32),
                pltpu.VMEM((2 * outer, queries, own // 2), f32),
                pltpu.VMEM((2 * outer, queries, own // 2), f32),
                pltpu.VMEM((2 * far, queries, own // 2), f32),
                pltpu.VMEM((2 * far, queries, own // 2), f32),
                pltpu.VMEM((group, 4, stat_lanes), f32),
                pltpu.VMEM((group, rows, cols), f32),
                pltpu.VMEM((group, rows, cols), f32),
                pltpu.VMEM((rows, cols), f32),
                pltpu.VMEM((queries, own), bf16),
                dma((7 + widths,)),
                dma((blocks,)),
                dma((blocks,)),
                dma((blocks,)),
                dma((blocks,)),
                dma((2 * outer,)),
                dma((2 * outer,)),
                dma((2 * far,)),
                dma((2 * far,)),
                dma((1,)),
                dma((1,)),
                dma((1,)),
                dma((1,)),
                dma((widths,)),
                dma((widths,)),
            ],
            compiler_params=pltpu.CompilerParams(
                collective_id=0, has_side_effects=True, vmem_limit_bytes=60 * 1024 * 1024
            ),
        )(
            t_query,
            t_pass,
            s_query,
            s_pass,
            positive.reshape(1, queries),
            doc_ids.reshape(lines, LANES),
        )
        s_scale = TEMPER / math.sqrt(s_width)
        grad_passage = s_scale * lax.dot_general(
            slope, queries_all.reshape(queries, s_width), TN, preferred_element_type=f32
        )
        if not whole_tiles:
            pieces = grad_query.reshape(outer, 2, rows, cols)
            grad_query = pieces.transpose(1, 2, 0, 3).reshape(panel, s_width)
        return grad_query, grad_passage

    placed = (
        P(("groups", "blk"), "width"),
        P(("groups", "blk"), "width"),
        P(("groups", "blk"), None),
        P(("groups", "blk", "width"), None),
        P("groups"),
        P("groups"),
    )
    return jax.shard_map(
        body,
        mesh=mesh,
        in_specs=placed,
        out_specs=(P(("groups", "blk"), None), P(("groups", "blk", "width"), None)),
        check_vma=False,
    )
```
